32 devices in a mesh: vocab: 4 (over y, core), dp: 2 (over x), replica: 4 (over z).
Axes of the slice: x: 2, y: 2, z: 4, core: 2. Of those that a mesh axis runs over, the one named last changes fastest.
Arguments:
- hidden: bfloat16 [256, 4096], P('dp'), may hold values from -6 to 6
- head_weight: bfloat16 [4096, 16384], P('dp', ('vocab', 'replica')), may hold values from -0.09375 to 0.09375
- head_bias: float32 [16384], P(('vocab', 'replica')), may hold values from -2.5 to 2.5
- rep_cotangent: float32 [16, 16384], P('dp', ('vocab', 'replica')), may hold values from -6 to 6
- lengths: int32 [16], P('dp'), may hold values from 1 to 16, 160 in all
Outputs:
- pooled: float32 [16, 16384], P('dp', ('vocab', 'replica'))
- term_mean: float32 [16384], P(('vocab', 'replica'))
- bias_grad: float32 [16384], P(('vocab', 'replica'))
- weight_grad: float32 [4096, 16384], P('dp', ('vocab', 'replica'))
- input_grad: float32 [256, 4096], P(('vocab', 'replica'), 'dp')
The draws below stay inside these ranges and needn't reach their ends.
Inputs may be any that keep to these rules, and one draw needn't show every extreme that they name: `lengths`: each sequence has at least one live token; some sequence has all 16 live.
All inputs are finite; a program needn't handle non-finite values. No bound on the sum of `lengths` on one device may be relied on, other than what follows from the above.
Results may differ from the reference program's by a relative error of at most 0.015.
Values may be sent and summed in bfloat16 or wider, within the bound.
A program may use at most 64 MiB of HBM per device.

```python
import math
import jax
import jax.numpy as jnp
import numpy as np
from jax import lax

D = 4096
LEN = 16
VOCAB = 16384
SEQS = 16
TOKENS = 256
N_DP = 2


def levels(rng, shape, cuts, least, top_value):
    def one(dim, shards_of):
        heights = jax.random.uniform(jax.random.fold_in(jax.random.fold_in(rng, 6), dim), (shards_of,), jnp.float32, least / len(cuts), top_value / len(cuts))
        return jnp.repeat(jnp.exp(heights), shape[dim] // shards_of).reshape((-1,) + (1,) * (len(shape) - dim - 1))

    factor_of = one(*cuts[0])
    for cut in cuts[1:]:
        factor_of = factor_of * one(*cut)
    return factor_of


def profile(amount, total, reach, lean):
    portions = [(1 << 20) // math.isqrt(standing ** lean) + 1 for standing in range(2, amount + 1)]
    surplus, holding = total - reach - (amount - 1), [1] * (amount - 1)
    while surplus > 0:
        movable = [i for i in range(amount - 1) if holding[i] < reach]
        mass, left = sum([portions[i] for i in movable]), surplus
        for i in movable:
            more = min(reach - holding[i], max(1, left * portions[i] // mass), surplus)
            holding[i] = holding[i] + more
            surplus = surplus - more
    return np.array([reach] + holding)


def ragged_sizes(stream_key, amount, total, limit, slope):
    if amount == 2:
        one = jax.random.randint(stream_key, (), max(1, total - limit), min(limit, total - 1) + 1)
        return jnp.stack([one, total - one])
    sizes = jnp.asarray(profile(amount, total, limit, slope), jnp.int32)
    couples = (amount - 1) // 2
    giver, receiver = sizes[1:1 + 2 * couples:2], sizes[2:2 + 2 * couples:2]
    slack = jnp.minimum(giver - 1, limit - receiver)
    shifted = jax.random.randint(jax.random.fold_in(stream_key, 1), (couples,), 0, 1 << 20) % (slack + 1)
    sizes = sizes.at[1:1 + 2 * couples:2].set(giver - shifted).at[2:2 + 2 * couples:2].set(receiver + shifted)
    return sizes[jax.random.permutation(jax.random.fold_in(stream_key, 2), amount)]


def normal_values(stream_key, extent, width, most, cuts=(), kind=jnp.bfloat16):
    factor_of = levels(stream_key, extent, cuts, -0.22, 0.18) if cuts else 1.0
    array = jax.random.normal(stream_key, extent, jnp.float32) * width * factor_of
    return jnp.minimum(jnp.maximum(array, -most), most).astype(kind)


def setup_inputs(seed: int = 0) -> dict:
    key_of = jax.random.split(jax.random.key(seed), 6)
    hidden = normal_values(key_of[0], (TOKENS, D), 1.0, 6.0, ((0, 2),))
    head_weight = normal_values(key_of[1], (D, VOCAB), D ** -0.5, 0.09375, ((0, 2), (1, 16)))
    head_bias = normal_values(key_of[2], (VOCAB,), 0.5, 2.5, ((0, 16),), jnp.float32)
    rep_cotangent = normal_values(key_of[3], (SEQS, VOCAB), 1.0, 6.0, ((0, 2), (1, 16)), jnp.float32)
    lengths = ragged_sizes(key_of[4], SEQS, SEQS * LEN * 5 // 8, LEN, 2).astype(jnp.int32)
    return {"hidden": hidden, "head_weight": head_weight, "head_bias": head_bias, "rep_cotangent": rep_cotangent, "lengths": lengths}


def reference(hidden, head_weight, head_bias, rep_cotangent, lengths):
    block = D // N_DP
    logits = jnp.zeros((TOKENS, VOCAB), jnp.float32)
    for index in range(N_DP):
        part = jnp.dot(hidden[:, index * block:(index + 1) * block], head_weight[index * block:(index + 1) * block, :], preferred_element_type=jnp.float32).astype(jnp.bfloat16)
        logits = logits + lax.optimization_barrier(part).astype(jnp.float32)
    logits = logits + head_bias[None, :]
    positive = jnp.maximum(logits, 0.0)
    act = jnp.log1p(positive)
    grid = act.reshape(SEQS, LEN, VOCAB)
    live = (jnp.arange(LEN, dtype=jnp.int32)[None, :] < lengths[:, None]).astype(jnp.float32)[:, :, None]
    squared = grid * grid
    total = 1.0 + jnp.sum(live * squared * squared, axis=1)
    pooled = total ** 0.25 - 1.0
    term_mean = jnp.sum(pooled, axis=0) / SEQS
    grad_pooled = rep_cotangent + term_mean[None, :]
    factor = live * squared * grid * (total ** -0.75)[:, None, :] / (1.0 + positive.reshape(SEQS, LEN, VOCAB))
    grad_logits = (factor * grad_pooled[:, None, :]).reshape(TOKENS, VOCAB)
    bias_grad = jnp.sum(grad_logits, axis=0)
    grad_round = grad_logits.astype(jnp.bfloat16)
    weight_grad = jnp.dot(hidden.T, grad_round, preferred_element_type=jnp.float32)
    input_grad = jnp.dot(grad_round, head_weight.T, preferred_element_type=jnp.float32)
    return (pooled, term_mean, bias_grad, weight_grad, input_grad)
```

```python
import jax
import jax.numpy as jnp
from jax import lax
from jax.sharding import PartitionSpec as P


def per_device(hidden, head_weight, head_bias, rep_cotangent, lengths):
    dp_count = lax.axis_size("dp")
    vocab_cols = head_weight.shape[1]
    columns = lax.all_to_all(hidden, "dp", split_axis=1, concat_axis=0, tiled=True)
    rep_all = lax.all_gather(rep_cotangent, "dp", axis=0, tiled=True)
    lengths_all = lax.all_gather(lengths.astype(jnp.float32), "dp", axis=0, tiled=True)
    seq_count = lengths_all.shape[0]
    tok_rows = columns.shape[0]
    seq_len = tok_rows // seq_count
    part = jnp.dot(columns, head_weight, preferred_element_type=jnp.float32).astype(jnp.bfloat16)
    part = lax.optimization_barrier(part)
    if dp_count == 2:
        other = lax.ppermute(part, "dp", [(0, 1), (1, 0)])
        running = part.astype(jnp.float32) + other.astype(jnp.float32)
    else:
        parts = lax.all_gather(part, "dp", axis=0, tiled=False)
        running = jnp.sum(parts.astype(jnp.float32), axis=0)
    logits = running + head_bias[None, :]
    positive = jnp.maximum(logits, 0.0)
    grid = jnp.log1p(positive).reshape(seq_count, seq_len, vocab_cols)
    slot = jnp.arange(seq_len, dtype=jnp.float32)
    live = (slot[None, :] < lengths_all[:, None]).astype(jnp.float32)[:, :, None]
    squared = grid * grid
    total = 1.0 + jnp.sum(live * squared * squared, axis=1)
    pooled = total**0.25 - 1.0
    factor = (
        live * squared * grid * (total ** (-0.75))[:, None, :]
        / (1.0 + positive.reshape(seq_count, seq_len, vocab_cols))
    )
    term_mean = jnp.sum(pooled, axis=0) / seq_count
    grad_pooled = rep_all + term_mean[None, :]
    grad_logits = (factor * grad_pooled[:, None, :]).reshape(tok_rows, vocab_cols)
    bias_grad = jnp.sum(grad_logits, axis=0)
    grad_round = grad_logits.astype(jnp.bfloat16)
    input_part = jnp.einsum("tv,kv->tk", grad_round, head_weight, preferred_element_type=jnp.float32)
    input_grad = lax.psum_scatter(input_part, ("vocab", "replica"), scatter_dimension=0, tiled=True)
    weight_grad = jnp.einsum("tk,tv->kv", columns, grad_round, preferred_element_type=jnp.float32)
    own = seq_count // dp_count
    pooled_own = lax.dynamic_slice_in_dim(pooled, lax.axis_index("dp") * own, own, 0)
    return (pooled_own, term_mean, bias_grad, weight_grad, input_grad)


def solution(mesh):
    placed = (
        P("dp", None),
        P("dp", ("vocab", "replica")),
        P(("vocab", "replica")),
        P("dp", ("vocab", "replica")),
        P("dp"),
    )
    return jax.shard_map(
        per_device,
        mesh=mesh,
        in_specs=placed,
        out_specs=(
            P("dp", ("vocab", "replica")),
            P(("vocab", "replica")),
            P(("vocab", "replica")),
            P("dp", ("vocab", "replica")),
            P(("vocab", "replica"), "dp"),
        ),
        check_vma=False,
    )
```

```python
import jax
import jax.numpy as jnp
from jax import lax
from jax.experimental import pallas as pl
from jax.experimental.pallas import tpu as pltpu
from jax.sharding import PartitionSpec as P


def per_device(hidden, head_weight, head_bias, rep_cotangent, lengths):
    dp_count = lax.axis_size("dp")
    vocab_cols = head_weight.shape[1]
    columns = lax.all_to_all(hidden, "dp", split_axis=1, concat_axis=0, tiled=True)
    rep_all = lax.all_gather(rep_cotangent, "dp", axis=0, tiled=True)
    lengths_all = lax.all_gather(lengths.astype(jnp.float32), "dp", axis=0, tiled=True)
    seq_count = lengths_all.shape[0]
    tok_rows = columns.shape[0]
    seq_len = tok_rows // seq_count
    part = jnp.dot(columns, head_weight, preferred_element_type=jnp.float32).astype(jnp.bfloat16)
    part = lax.optimization_barrier(part)
    if dp_count == 2:
        other = lax.ppermute(part, "dp", [(0, 1), (1, 0)])
        running = part.astype(jnp.float32) + other.astype(jnp.float32)
    else:
        parts = lax.all_gather(part, "dp", axis=0, tiled=False)
        running = jnp.sum(parts.astype(jnp.float32), axis=0)
    logits = running + head_bias[None, :]
    positive = jnp.maximum(logits, 0.0)
    grid = jnp.log1p(positive).reshape(seq_count, seq_len, vocab_cols)
    slot = jnp.arange(seq_len, dtype=jnp.float32)
    live = (slot[None, :] < lengths_all[:, None]).astype(jnp.float32)[:, :, None]
    squared = grid * grid
    total = 1.0 + jnp.sum(live * squared * squared, axis=1)
    pooled = total**0.25 - 1.0
    factor = (
        live * squared * grid * (total ** (-0.75))[:, None, :]
        / (1.0 + positive.reshape(seq_count, seq_len, vocab_cols))
    )
    term_mean = jnp.sum(pooled, axis=0) / seq_count
    grad_pooled = rep_all + term_mean[None, :]
    grad_logits = (factor * grad_pooled[:, None, :]).reshape(tok_rows, vocab_cols)
    bias_grad = jnp.sum(grad_logits, axis=0)
    grad_round = grad_logits.astype(jnp.bfloat16)
    input_part = jnp.einsum("tv,kv->tk", grad_round, head_weight, preferred_element_type=jnp.float32)
    input_grad = lax.psum_scatter(input_part, ("vocab", "replica"), scatter_dimension=0, tiled=True)
    weight_grad = jnp.einsum("tk,tv->kv", columns, grad_round, preferred_element_type=jnp.float32)
    own = seq_count // dp_count
    pooled_own = lax.dynamic_slice_in_dim(pooled, lax.axis_index("dp") * own, own, 0)
    return (pooled_own, term_mean, bias_grad, weight_grad, input_grad)


NC = 4
MESH = pl.DeviceIdType.MESH


def head_kernel(
    hidden, weight, bias, replen,
    pooled_out, mean_out, biasg_out, cols_out, grad_out, inp_out,
    wv, xall, rl, prt, rpt, factor, pool, grad, ipf, s1, r1, k2, s2, r2, k3, s3, r3,
    w_sem, hs_send, hs_recv, fw_send, fw_recv, rl_send, rl_recv, pt_send, pt_recv,
    c_send, c_recv, y_send, y_recv, z_send, z_recv,
):
    v, d, rz = lax.axis_index("vocab"), lax.axis_index("dp"), lax.axis_index("replica")
    p = 1 - d
    b, a = lax.rem(v, 2), v // 2
    sib = {"vocab": v + 1 - 2 * b}
    yp = {"vocab": lax.rem(v + 2, 4)}
    dpp = {"dp": p}
    half = hidden.shape[1] // 2
    cw = half // NC
    vw = wv.shape[1] // NC
    rows = hidden.shape[0]
    seqs = rl.shape[1]
    slen = rows // seqs
    hr = rows // 4

    def remote(src, dst, ss, rs, dev):
        return pltpu.make_async_remote_copy(
            src_ref=src, dst_ref=dst, send_sem=ss, recv_sem=rs, device_id=dev, device_id_type=MESH
        )

    loads = []
    for c in range(NC):
        cp = pltpu.make_async_copy(
            weight.at[:, pl.ds(c * vw, vw)], wv.at[:, pl.ds(c * vw, vw)], w_sem.at[c]
        )
        cp.start()
        loads.append(cp)
    barrier = pltpu.get_barrier_semaphore()
    zps = [{"replica": lax.rem(rz + j, 4)} for j in (1, 2, 3)]
    for dev in [sib, yp, dpp] + zps:
        pl.semaphore_signal(barrier, inc=1, device_id=dev, device_id_type=MESH)
    pl.semaphore_wait(barrier, 6)

    pend = []
    hcopies = []
    for q in range(2):
        rr = pl.ds(pl.multiple_of(b * (2 * hr) + q * hr, hr), hr)
        cp = remote(
            hidden.at[rr, pl.ds(pl.multiple_of(p * half, half), half)],
            xall.at[d, rr], hs_send.at[q], hs_recv.at[q], dpp,
        )
        cp.start()
        hcopies.append(cp)
    rlc = remote(replen, rl.at[d], rl_send, rl_recv, dpp)
    rlc.start()
    pend += hcopies + [rlc]
    rl[d] = replen[...]
    xall[d] = hidden[:, pl.ds(pl.multiple_of(d * half, half), half)]

    def parts(h, ph):
        out = []
        for c in range(NC):
            if ph == 0:
                loads[c].wait()
            prt[h, c] = jnp.dot(
                xall[h], wv[:, c * vw : (c + 1) * vw], preferred_element_type=jnp.float32
            ).astype(jnp.bfloat16)
            cp = remote(prt.at[h, c], rpt.at[h, c], pt_send.at[ph, c], pt_recv.at[ph, c], dpp)
            cp.start()
            out.append(cp)
        return out

    own_parts = parts(d, 0)
    fws = []
    for q in range(2):
        hcopies[q].wait_recv()
        rr = pl.ds(pl.multiple_of(b * (2 * hr) + q * hr, hr), hr)
        cp = remote(xall.at[p, rr], xall.at[p, rr], fw_send.at[q], fw_recv.at[q], sib)
        cp.start()
        fws.append(cp)
    for cp in fws:
        cp.wait_recv()
    other_parts = parts(p, 1)
    pend += fws + own_parts + other_parts
    rlc.wait_recv()

    slot = lax.broadcasted_iota(jnp.int32, (seqs, slen, vw), 1).astype(jnp.float32)

    def forward(h, c):
        x = prt[h, c].astype(jnp.float32) + rpt[h, c].astype(jnp.float32)
        x = x + bias[:, c * vw : (c + 1) * vw]
        pos = jnp.maximum(x, 0.0)
        act = jnp.log1p(pos).reshape(seqs, slen, vw)
        lens = rl[h, :, wv.shape[1] :]
        live = slot < lens[:, None, :]
        act = jnp.where(live, act, 0.0)
        sq = act * act
        total = 1.0 + jnp.sum(sq * sq, axis=1)
        root = jnp.sqrt(jnp.sqrt(total))
        pool[h, c] = root - 1.0
        inv = 1.0 / root
        inv3 = inv * inv * inv
        f = sq * act * inv3[:, None, :] / (1.0 + pos.reshape(seqs, slen, vw))
        factor[h, c] = f.reshape(rows, vw)

    for c in range(NC):
        own_parts[c].wait_recv()
        forward(p, c)
    for c in range(NC):
        other_parts[c].wait_recv()
        forward(d, c)
        cs = slice(c * vw, (c + 1) * vw)
        mean = (
            jnp.sum(pool[0, c], axis=0, keepdims=True) + jnp.sum(pool[1, c], axis=0, keepdims=True)
        ) / (2 * seqs)
        mean_out[:, cs] = mean
        pooled_out[:, cs] = pool[d, c]
        bsum = jnp.zeros((1, vw), jnp.float32)
        for h in range(2):
            gp = rl[h, :, cs] + mean
            g = (factor[h, c].reshape(seqs, slen, vw) * gp[:, None, :]).reshape(rows, vw)
            bsum = bsum + jnp.sum(g, axis=0, keepdims=True)
            grad[h, :, cs] = g.astype(jnp.bfloat16)
        biasg_out[:, cs] = bsum

    vr = 2 * rows // 4
    zr = vr // 4
    cc, yy, zz = [], [], []
    for c in range(NC):
        res = lax.dot_general(
            grad[...].reshape(2 * rows, NC * vw), wv[c * cw : (c + 1) * cw, :],
            (((1,), (1,)), ((), ())), preferred_element_type=jnp.float32,
        )
        for u in range(4):
            blk = res[u * vr : (u + 1) * vr]
            ipf[c, u % 2, u // 2] = blk
            s1[c, u % 2, u // 2] = blk.astype(jnp.bfloat16)
        cp = remote(s1.at[c, 1 - b], r1.at[c], c_send.at[c], c_recv.at[c], sib)
        cp.start()
        cc.append(cp)
    for c in range(NC):
        cc[c].wait_recv()
        s2[c] = (ipf[c, b, 1 - a] + r1[c, 1 - a].astype(jnp.float32)).astype(jnp.bfloat16)
        cp = remote(s2.at[c], r2.at[c], y_send.at[c], y_recv.at[c], yp)
        cp.start()
        yy.append(cp)
        k2[c] = ipf[c, b, a] + r1[c, a].astype(jnp.float32)
    cols_out[...] = xall[...]
    grad_out[...] = grad[...]
    for c in range(NC):
        yy[c].wait_recv()
        tot = (k2[c] + r2[c].astype(jnp.float32)).reshape(4, zr, cw)
        k3[c] = tot
        s3[c] = tot.astype(jnp.bfloat16)
        row = []
        for j in (1, 2, 3):
            to = lax.rem(rz + j, 4)
            cp = remote(
                s3.at[c, to], r3.at[c, j - 1], z_send.at[c, j - 1], z_recv.at[c, j - 1],
                {"replica": to},
            )
            cp.start()
            row.append(cp)
        zz.append(row)
    for c in range(NC):
        tot = k3[c, rz]
        for j in range(3):
            zz[c][j].wait_recv()
            tot = tot + r3[c, j].astype(jnp.float32)
        inp_out[:, c * cw : (c + 1) * cw] = tot
    for cp in pend + cc + yy + sum(zz, []):
        cp.wait_send()


def weight_kernel(cols, grad, out):
    out[...] = lax.dot_general(
        cols[...], grad[...], (((0,), (0,)), ((), ())), preferred_element_type=jnp.float32
    )


def fused(hidden, head_weight, head_bias, rep_cotangent, lengths):
    rows, width = hidden.shape
    half, vc = head_weight.shape
    seqs = lengths.shape[0]
    vw, cw = vc // NC, half // NC
    vr = 2 * rows // 4
    zr = vr // 4
    bf, f32 = jnp.bfloat16, jnp.float32
    wide = jnp.broadcast_to(lengths.astype(f32)[:, None], (seqs, vw))
    replen = jnp.concatenate([rep_cotangent, wide], axis=1)
    vm = pl.BlockSpec(memory_space=pltpu.VMEM)
    dma = pltpu.SemaphoreType.DMA
    sds = jax.ShapeDtypeStruct
    pooled, mean, biasg, cols, grad, inp = pl.pallas_call(
        head_kernel,
        out_shape=(
            sds((seqs, vc), f32), sds((1, vc), f32), sds((1, vc), f32),
            sds((2, rows, half), bf), sds((2, rows, vc), bf), sds((zr, half), f32),
        ),
        in_specs=[vm, pl.BlockSpec(memory_space=pl.ANY), vm, vm],
        out_specs=(vm,) * 6,
        scratch_shapes=[
            pltpu.VMEM((half, vc), bf),
            pltpu.VMEM((2, rows, half), bf),
            pltpu.VMEM((2, seqs, vc + vw), f32),
            pltpu.VMEM((2, NC, rows, vw), bf),
            pltpu.VMEM((2, NC, rows, vw), bf),
            pltpu.VMEM((2, NC, rows, vw), f32),
            pltpu.VMEM((2, NC, seqs, vw), f32),
            pltpu.VMEM((2, rows, vc), bf),
            pltpu.VMEM((NC, 2, 2, vr, cw), f32),
            pltpu.VMEM((NC, 2, 2, vr, cw), bf),
            pltpu.VMEM((NC, 2, vr, cw), bf),
            pltpu.VMEM((NC, vr, cw), f32),
            pltpu.VMEM((NC, vr, cw), bf),
            pltpu.VMEM((NC, vr, cw), bf),
            pltpu.VMEM((NC, 4, zr, cw), f32),
            pltpu.VMEM((NC, 4, zr, cw), bf),
            pltpu.VMEM((NC, 3, zr, cw), bf),
            dma((NC,)), dma((2,)), dma((2,)), dma((2,)), dma((2,)), dma, dma,
            dma((2, NC)), dma((2, NC)), dma((NC,)), dma((NC,)), dma((NC,)), dma((NC,)),
            dma((NC, 3)), dma((NC, 3)),
        ],
        compiler_params=pltpu.CompilerParams(
            collective_id=0, has_side_effects=True, vmem_limit_bytes=44 * 1024 * 1024
        ),
    )(hidden, head_weight, head_bias[None, :], replen)
    kb = 256
    weight_grad = pl.pallas_call(
        weight_kernel,
        grid=(half // kb,),
        out_shape=sds((half, vc), f32),
        in_specs=[
            pl.BlockSpec((2 * rows, kb), lambda i: (0, i)),
            pl.BlockSpec((2 * rows, vc), lambda i: (0, 0)),
        ],
        out_specs=pl.BlockSpec((kb, vc), lambda i: (i, 0)),
        compiler_params=pltpu.CompilerParams(vmem_limit_bytes=24 * 1024 * 1024),
    )(cols.reshape(2 * rows, half), grad.reshape(2 * rows, vc))
    return (pooled, mean[0], biasg[0], weight_grad, inp)


def solution(mesh):
    small = mesh.shape["dp"] == 2 and mesh.shape["vocab"] == 4 and mesh.shape["replica"] == 4
    placed = (
        P("dp", None),
        P("dp", ("vocab", "replica")),
        P(("vocab", "replica")),
        P("dp", ("vocab", "replica")),
        P("dp"),
    )
    return jax.shard_map(
        fused if small else per_device,
        mesh=mesh,
        in_specs=placed,
        out_specs=(
            P("dp", ("vocab", "replica")),
            P(("vocab", "replica")),
            P(("vocab", "replica")),
            P("dp", ("vocab", "replica")),
            P(("vocab", "replica"), "dp"),
        ),
        check_vma=False,
    )
```

```python
import jax
import jax.numpy as jnp
from jax import lax
from jax.experimental import pallas as pl
from jax.experimental.pallas import tpu as pltpu
from jax.sharding import PartitionSpec as P


def per_device(hidden, head_weight, head_bias, rep_cotangent, lengths):
    dp_count = lax.axis_size("dp")
    vocab_cols = head_weight.shape[1]
    columns = lax.all_to_all(hidden, "dp", split_axis=1, concat_axis=0, tiled=True)
    rep_all = lax.all_gather(rep_cotangent, "dp", axis=0, tiled=True)
    lengths_all = lax.all_gather(lengths.astype(jnp.float32), "dp", axis=0, tiled=True)
    seq_count = lengths_all.shape[0]
    tok_rows = columns.shape[0]
    seq_len = tok_rows // seq_count
    part = jnp.dot(columns, head_weight, preferred_element_type=jnp.float32).astype(jnp.bfloat16)
    part = lax.optimization_barrier(part)
    if dp_count == 2:
        other = lax.ppermute(part, "dp", [(0, 1), (1, 0)])
        running = part.astype(jnp.float32) + other.astype(jnp.float32)
    else:
        parts = lax.all_gather(part, "dp", axis=0, tiled=False)
        running = jnp.sum(parts.astype(jnp.float32), axis=0)
    logits = running + head_bias[None, :]
    positive = jnp.maximum(logits, 0.0)
    grid = jnp.log1p(positive).reshape(seq_count, seq_len, vocab_cols)
    slot = jnp.arange(seq_len, dtype=jnp.float32)
    live = (slot[None, :] < lengths_all[:, None]).astype(jnp.float32)[:, :, None]
    squared = grid * grid
    total = 1.0 + jnp.sum(live * squared * squared, axis=1)
    pooled = total**0.25 - 1.0
    factor = (
        live * squared * grid * (total ** (-0.75))[:, None, :]
        / (1.0 + positive.reshape(seq_count, seq_len, vocab_cols))
    )
    term_mean = jnp.sum(pooled, axis=0) / seq_count
    grad_pooled = rep_all + term_mean[None, :]
    grad_logits = (factor * grad_pooled[:, None, :]).reshape(tok_rows, vocab_cols)
    bias_grad = jnp.sum(grad_logits, axis=0)
    grad_round = grad_logits.astype(jnp.bfloat16)
    input_part = jnp.einsum("tv,kv->tk", grad_round, head_weight, preferred_element_type=jnp.float32)
    input_grad = lax.psum_scatter(input_part, ("vocab", "replica"), scatter_dimension=0, tiled=True)
    weight_grad = jnp.einsum("tk,tv->kv", columns, grad_round, preferred_element_type=jnp.float32)
    own = seq_count // dp_count
    pooled_own = lax.dynamic_slice_in_dim(pooled, lax.axis_index("dp") * own, own, 0)
    return (pooled_own, term_mean, bias_grad, weight_grad, input_grad)


NC = 4
MESH = pl.DeviceIdType.MESH


def head_kernel(
    hidden, weight, bias_in, replen, lengths,
    pooled_out, mean_out, biasg_out, cols_out, grad_out, inp_out,
    wv, bias, xall, xt, rl, ln, prt, rpt, factor, pool, grad, ipf, s1, r1, k2, s2, r2, k3, s3, r3,
    w_sem, l_sem, o_sem, hs_send, hs_recv, fw_send, fw_recv, fy_send, fy_recv, ys_send, ys_recv, ln_send, ln_recv, rl_send, rl_recv, pt_send, pt_recv,
    c_send, c_recv, y_send, y_recv, z_send, z_recv,
):
    v, d, rz = lax.axis_index("vocab"), lax.axis_index("dp"), lax.axis_index("replica")
    p = 1 - d
    b, a = lax.rem(v, 2), v // 2
    sib = {"vocab": v + 1 - 2 * b}
    yp = {"vocab": lax.rem(v + 2, 4)}
    dpp = {"dp": p}
    half = hidden.shape[1] // 2
    cw = half // NC
    vw = wv.shape[1] // NC
    rows = hidden.shape[0]
    seqs = rl.shape[1]
    slen = rows // seqs
    hr = rows // 8

    def remote(src, dst, ss, rs, dev):
        return pltpu.make_async_remote_copy(
            src_ref=src, dst_ref=dst, send_sem=ss, recv_sem=rs, device_id=dev, device_id_type=MESH
        )

    firsts = [
        pltpu.make_async_copy(
            hidden.at[:, pl.ds(pl.multiple_of(d * half, half), half)], xall.at[d], l_sem.at[0]
        ),
        pltpu.make_async_copy(replen, rl.at[d], l_sem.at[1]),
        pltpu.make_async_copy(bias_in, bias, l_sem.at[2]),
    ]
    for cp in firsts:
        cp.start()
    for i in range(seqs):
        ln[d, i : i + 1, :] = jnp.full((1, vw), lengths[i].astype(jnp.float32))
    loads = []
    for c in range(NC):
        cp = pltpu.make_async_copy(
            weight.at[:, pl.ds(c * vw, vw)], wv.at[:, pl.ds(c * vw, vw)], w_sem.at[c]
        )
        cp.start()
        loads.append(cp)
    barrier = pltpu.get_barrier_semaphore()
    zps = [{"replica": lax.rem(rz + j, 4)} for j in (1, 2, 3)]
    for dev in [sib, yp, dpp] + zps:
        pl.semaphore_signal(barrier, inc=1, device_id=dev, device_id_type=MESH)
    pl.semaphore_wait(barrier, 6)

    pend = []
    hcopies = []

    def piece(who, q):
        return pl.ds(pl.multiple_of(who * (2 * hr) + q * hr, hr), hr)

    for q in range(2):
        cp = remote(
            hidden.at[piece(v, q), pl.ds(pl.multiple_of(p * half, half), half)],
            xall.at[d, piece(v, q)], hs_send.at[q], hs_recv.at[q], dpp,
        )
        cp.start()
        hcopies.append(cp)
    rlc = remote(replen, rl.at[d], rl_send, rl_recv, dpp)
    rlc.start()
    lnc = remote(ln.at[d], ln.at[d], ln_send, ln_recv, dpp)
    lnc.start()
    pend += hcopies + [rlc, lnc]
    for cp in firsts:
        cp.wait()

    def parts(h, ph):
        out = []
        for c in range(NC):
            if ph == 0:
                loads[c].wait()
            prt[h, c] = jnp.dot(
                xall[h], wv[:, c * vw : (c + 1) * vw], preferred_element_type=jnp.float32
            ).astype(jnp.bfloat16)
            cp = remote(prt.at[h, c], rpt.at[h, c], pt_send.at[ph, c], pt_recv.at[ph, c], dpp)
            cp.start()
            out.append(cp)
        return out

    own_parts = parts(d, 0)
    fws, fys, fyy = [], [], []
    yv = lax.rem(v + 2, 4)
    for q in range(2):
        hcopies[q].wait_recv()
        src = xall.at[p, piece(v, q)]
        cp = remote(src, src, fy_send.at[q], fy_recv.at[q], yp)
        cp.start()
        fyy.append(cp)
        cp = remote(src, src, fw_send.at[q], fw_recv.at[q], sib)
        cp.start()
        fws.append(cp)
    for q in range(2):
        fyy[q].wait_recv()
        src = xall.at[p, piece(yv, q)]
        cp = remote(src, src, ys_send.at[q], ys_recv.at[q], sib)
        cp.start()
        fys.append(cp)
    for cp in fws + fys:
        cp.wait_recv()
    other_parts = parts(p, 1)
    pend += fws + fys + fyy + own_parts + other_parts
    rlc.wait_recv()
    lnc.wait_recv()
    for h in range(2):
        for k in range(NC):
            ks = slice(k * cw, (k + 1) * cw)
            xt[ks, h * rows : (h + 1) * rows] = xall[h, :, ks].T
    cols_copy = pltpu.make_async_copy(xt, cols_out, o_sem.at[0])
    cols_copy.start()

    slot = lax.broadcasted_iota(jnp.int32, (seqs, slen, vw), 1).astype(jnp.float32)

    def forward(h, c):
        x = prt[h, c].astype(jnp.float32) + rpt[h, c].astype(jnp.float32)
        x = x + bias[:, c * vw : (c + 1) * vw]
        pos = jnp.maximum(x, 0.0)
        act = jnp.log1p(pos).reshape(seqs, slen, vw)
        lens = ln[h]
        live = slot < lens[:, None, :]
        act = jnp.where(live, act, 0.0)
        sq = act * act
        total = 1.0 + jnp.sum(sq * sq, axis=1)
        root = jnp.sqrt(jnp.sqrt(total))
        pool[h, c] = root - 1.0
        inv = 1.0 / root
        inv3 = inv * inv * inv
        f = sq * act * inv3[:, None, :] / (1.0 + pos.reshape(seqs, slen, vw))
        factor[h, c] = f.reshape(rows, vw)

    for c in range(NC):
        own_parts[c].wait_recv()
        forward(p, c)
    for c in range(NC):
        other_parts[c].wait_recv()
        forward(d, c)
        cs = slice(c * vw, (c + 1) * vw)
        mean = (
            jnp.sum(pool[0, c], axis=0, keepdims=True) + jnp.sum(pool[1, c], axis=0, keepdims=True)
        ) / (2 * seqs)
        mean_out[:, cs] = mean
        pooled_out[:, cs] = pool[d, c]
        bsum = jnp.zeros((1, vw), jnp.float32)
        for h in range(2):
            gp = rl[h, :, cs] + mean
            g = (factor[h, c].reshape(seqs, slen, vw) * gp[:, None, :]).reshape(rows, vw)
            bsum = bsum + jnp.sum(g, axis=0, keepdims=True)
            grad[h, :, cs] = g.astype(jnp.bfloat16)
        biasg_out[:, cs] = bsum

    grad_copy = pltpu.make_async_copy(grad, grad_out, o_sem.at[1])
    grad_copy.start()
    vr = 2 * rows // 4
    zr = vr // 4
    cc, yy, zz = [], [], []
    for c in range(NC):
        res = lax.dot_general(
            grad[...].reshape(2 * rows, NC * vw), wv[c * cw : (c + 1) * cw, :],
            (((1,), (1,)), ((), ())), preferred_element_type=jnp.float32,
        )
        for u in range(4):
            blk = res[u * vr : (u + 1) * vr]
            ipf[c, u % 2, u // 2] = blk
            s1[c, u % 2, u // 2] = blk.astype(jnp.bfloat16)
        cp = remote(s1.at[c, 1 - b], r1.at[c], c_send.at[c], c_recv.at[c], sib)
        cp.start()
        cc.append(cp)
    for c in range(NC):
        cc[c].wait_recv()
        s2[c] = (ipf[c, b, 1 - a] + r1[c, 1 - a].astype(jnp.float32)).astype(jnp.bfloat16)
        cp = remote(s2.at[c], r2.at[c], y_send.at[c], y_recv.at[c], yp)
        cp.start()
        yy.append(cp)
        k2[c] = ipf[c, b, a] + r1[c, a].astype(jnp.float32)
    for c in range(NC):
        yy[c].wait_recv()
        tot = (k2[c] + r2[c].astype(jnp.float32)).reshape(4, zr, cw)
        k3[c] = tot
        s3[c] = tot.astype(jnp.bfloat16)
        row = []
        for j in (1, 2, 3):
            to = lax.rem(rz + j, 4)
            cp = remote(
                s3.at[c, to], r3.at[c, j - 1], z_send.at[c, j - 1], z_recv.at[c, j - 1],
                {"replica": to},
            )
            cp.start()
            row.append(cp)
        zz.append(row)
    for c in range(NC):
        tot = k3[c, rz]
        for j in range(3):
            zz[c][j].wait_recv()
            tot = tot + r3[c, j].astype(jnp.float32)
        inp_out[:, c * cw : (c + 1) * cw] = tot
    for cp in pend + cc + yy + sum(zz, []):
        cp.wait_send()
    cols_copy.wait()
    grad_copy.wait()


def weight_kernel(cols, grad, pooled, mean, biasg, inp, out, pooled_o, mean_o, biasg_o, inp_o):
    out[...] = jnp.dot(cols[...], grad[...], preferred_element_type=jnp.float32)

    @pl.when(pl.program_id(0) == 0)
    def _():
        pooled_o[...] = pooled[...]
        mean_o[...] = mean[...]
        biasg_o[...] = biasg[...]
        inp_o[...] = inp[...]


def fused(hidden, head_weight, head_bias, rep_cotangent, lengths):
    rows, width = hidden.shape
    half, vc = head_weight.shape
    seqs = lengths.shape[0]
    vw, cw = vc // NC, half // NC
    vr = 2 * rows // 4
    zr = vr // 4
    bf, f32 = jnp.bfloat16, jnp.float32
    vm = pl.BlockSpec(memory_space=pltpu.VMEM)
    hbm = pl.BlockSpec(memory_space=pl.ANY)
    dma = pltpu.SemaphoreType.DMA
    sds = jax.ShapeDtypeStruct
    pooled, mean, biasg, cols, grad, inp = pl.pallas_call(
        head_kernel,
        out_shape=(
            sds((seqs, vc), f32), sds((1, vc), f32), sds((1, vc), f32),
            sds((half, 2 * rows), bf), sds((2, rows, vc), bf), sds((zr, half), f32),
        ),
        in_specs=[hbm] * 4 + [pl.BlockSpec(memory_space=pltpu.SMEM)],
        out_specs=(vm, vm, vm, hbm, hbm, vm),
        scratch_shapes=[
            pltpu.VMEM((half, vc), bf),
            pltpu.VMEM((1, vc), f32),
            pltpu.VMEM((2, rows, half), bf),
            pltpu.VMEM((half, 2 * rows), bf),
            pltpu.VMEM((2, seqs, vc), f32),
            pltpu.VMEM((2, seqs, vw), f32),
            pltpu.VMEM((2, NC, rows, vw), bf),
            pltpu.VMEM((2, NC, rows, vw), bf),
            pltpu.VMEM((2, NC, rows, vw), f32),
            pltpu.VMEM((2, NC, seqs, vw), f32),
            pltpu.VMEM((2, rows, vc), bf),
            pltpu.VMEM((NC, 2, 2, vr, cw), f32),
            pltpu.VMEM((NC, 2, 2, vr, cw), bf),
            pltpu.VMEM((NC, 2, vr, cw), bf),
            pltpu.VMEM((NC, vr, cw), f32),
            pltpu.VMEM((NC, vr, cw), bf),
            pltpu.VMEM((NC, vr, cw), bf),
            pltpu.VMEM((NC, 4, zr, cw), f32),
            pltpu.VMEM((NC, 4, zr, cw), bf),
            pltpu.VMEM((NC, 3, zr, cw), bf),
            dma((NC,)), dma((3,)), dma((2,)), dma((2,)), dma((2,)), dma((2,)), dma((2,)),
            dma((2,)), dma((2,)), dma((2,)), dma((2,)), dma, dma, dma, dma,
            dma((2, NC)), dma((2, NC)), dma((NC,)), dma((NC,)), dma((NC,)), dma((NC,)),
            dma((NC, 3)), dma((NC, 3)),
        ],
        compiler_params=pltpu.CompilerParams(
            collective_id=0, has_side_effects=True, vmem_limit_bytes=60 * 1024 * 1024
        ),
    )(hidden, head_weight, head_bias[None, :], rep_cotangent, lengths)
    kb = 256
    small = (pooled, mean, biasg, inp)
    whole = [pl.BlockSpec(x.shape, lambda i: (0, 0)) for x in small]
    weight_grad, pooled, mean, biasg, inp = pl.pallas_call(
        weight_kernel,
        grid=(half // kb,),
        out_shape=[sds((half, vc), f32)] + [sds(x.shape, f32) for x in small],
        in_specs=[
            pl.BlockSpec((kb, 2 * rows), lambda i: (i, 0)),
            pl.BlockSpec((2 * rows, vc), lambda i: (0, 0)),
        ]
        + whole,
        out_specs=[pl.BlockSpec((kb, vc), lambda i: (i, 0))] + whole,
        compiler_params=pltpu.CompilerParams(vmem_limit_bytes=60 * 1024 * 1024),
    )(cols, grad.reshape(2 * rows, vc), *small)
    return (pooled, mean[0], biasg[0], weight_grad, inp)


def solution(mesh):
    small = mesh.shape["dp"] == 2 and mesh.shape["vocab"] == 4 and mesh.shape["replica"] == 4
    placed = (
        P("dp", None),
        P("dp", ("vocab", "replica")),
        P(("vocab", "replica")),
        P("dp", ("vocab", "replica")),
        P("dp"),
    )
    return jax.shard_map(
        fused if small else per_device,
        mesh=mesh,
        in_specs=placed,
        out_specs=(
            P("dp", ("vocab", "replica")),
            P(("vocab", "replica")),
            P(("vocab", "replica")),
            P("dp", ("vocab", "replica")),
            P(("vocab", "replica"), "dp"),
        ),
        check_vma=False,
    )
```

```python
import jax
import jax.numpy as jnp
from jax import lax
from jax.experimental import pallas as pl
from jax.experimental.pallas import tpu as pltpu
from jax.sharding import PartitionSpec as P


def per_device(hidden, head_weight, head_bias, rep_cotangent, lengths):
    dp_count = lax.axis_size("dp")
    vocab_cols = head_weight.shape[1]
    columns = lax.all_to_all(hidden, "dp", split_axis=1, concat_axis=0, tiled=True)
    rep_all = lax.all_gather(rep_cotangent, "dp", axis=0, tiled=True)
    lengths_all = lax.all_gather(lengths.astype(jnp.float32), "dp", axis=0, tiled=True)
    seq_count = lengths_all.shape[0]
    tok_rows = columns.shape[0]
    seq_len = tok_rows // seq_count
    part = jnp.dot(columns, head_weight, preferred_element_type=jnp.float32).astype(jnp.bfloat16)
    part = lax.optimization_barrier(part)
    if dp_count == 2:
        other = lax.ppermute(part, "dp", [(0, 1), (1, 0)])
        running = part.astype(jnp.float32) + other.astype(jnp.float32)
    else:
        parts = lax.all_gather(part, "dp", axis=0, tiled=False)
        running = jnp.sum(parts.astype(jnp.float32), axis=0)
    logits = running + head_bias[None, :]
    positive = jnp.maximum(logits, 0.0)
    grid = jnp.log1p(positive).reshape(seq_count, seq_len, vocab_cols)
    slot = jnp.arange(seq_len, dtype=jnp.float32)
    live = (slot[None, :] < lengths_all[:, None]).astype(jnp.float32)[:, :, None]
    squared = grid * grid
    total = 1.0 + jnp.sum(live * squared * squared, axis=1)
    pooled = total**0.25 - 1.0
    factor = (
        live * squared * grid * (total ** (-0.75))[:, None, :]
        / (1.0 + positive.reshape(seq_count, seq_len, vocab_cols))
    )
    term_mean = jnp.sum(pooled, axis=0) / seq_count
    grad_pooled = rep_all + term_mean[None, :]
    grad_logits = (factor * grad_pooled[:, None, :]).reshape(tok_rows, vocab_cols)
    bias_grad = jnp.sum(grad_logits, axis=0)
    grad_round = grad_logits.astype(jnp.bfloat16)
    input_part = jnp.einsum("tv,kv->tk", grad_round, head_weight, preferred_element_type=jnp.float32)
    input_grad = lax.psum_scatter(input_part, ("vocab", "replica"), scatter_dimension=0, tiled=True)
    weight_grad = jnp.einsum("tk,tv->kv", columns, grad_round, preferred_element_type=jnp.float32)
    own = seq_count // dp_count
    pooled_own = lax.dynamic_slice_in_dim(pooled, lax.axis_index("dp") * own, own, 0)
    return (pooled_own, term_mean, bias_grad, weight_grad, input_grad)


NC = 4
MESH = pl.DeviceIdType.MESH


def head_kernel(
    hidden, weight, bias_in, replen, lengths,
    pooled_out, mean_out, biasg_out, cols_out, grad_out, inp_out,
    wv, bias, xall, xt, rl, ln, prt, rpt, factor, pool, grad, ipf, s1, r1, k2, s2, r2, k3, s3, r3,
    w_sem, l_sem, o_sem, hs_send, hs_recv, fw_send, fw_recv, fy_send, fy_recv, ys_send, ys_recv, ln_send, ln_recv, rl_send, rl_recv, pt_send, pt_recv,
    c_send, c_recv, y_send, y_recv, z_send, z_recv,
):
    v, d, rz = lax.axis_index("vocab"), lax.axis_index("dp"), lax.axis_index("replica")
    p = 1 - d
    b, a = lax.rem(v, 2), v // 2
    sib = {"vocab": v + 1 - 2 * b}
    yp = {"vocab": lax.rem(v + 2, 4)}
    dpp = {"dp": p}
    half = hidden.shape[1] // 2
    cw = half // NC
    vw = wv.shape[1] // NC
    rows = hidden.shape[0]
    seqs = rl.shape[1]
    slen = rows // seqs
    hr = rows // 8

    def remote(src, dst, ss, rs, dev):
        return pltpu.make_async_remote_copy(
            src_ref=src, dst_ref=dst, send_sem=ss, recv_sem=rs, device_id=dev, device_id_type=MESH
        )

    firsts = [
        pltpu.make_async_copy(
            hidden.at[:, pl.ds(pl.multiple_of(d * half, half), half)], xall.at[d], l_sem.at[0]
        ),
        pltpu.make_async_copy(replen, rl.at[d], l_sem.at[1]),
        pltpu.make_async_copy(bias_in, bias, l_sem.at[2]),
    ]
    for cp in firsts:
        cp.start()
    for i in range(seqs):
        ln[d, i : i + 1, :] = jnp.full((1, vw), lengths[i].astype(jnp.float32))
    loads = []
    for c in range(NC):
        cp = pltpu.make_async_copy(
            weight.at[:, pl.ds(c * vw, vw)], wv.at[:, pl.ds(c * vw, vw)], w_sem.at[c]
        )
        cp.start()
        loads.append(cp)
    barrier = pltpu.get_barrier_semaphore()
    zps = [{"replica": lax.rem(rz + j, 4)} for j in (1, 2, 3)]
    for dev in [sib, yp, dpp] + zps:
        pl.semaphore_signal(barrier, inc=1, device_id=dev, device_id_type=MESH)
    pl.semaphore_wait(barrier, 6)

    pend = []
    hcopies = []

    def piece(who, q):
        return pl.ds(pl.multiple_of(who * (2 * hr) + q * hr, hr), hr)

    for q in range(2):
        cp = remote(
            hidden.at[piece(v, q), pl.ds(pl.multiple_of(p * half, half), half)],
            xall.at[d, piece(v, q)], hs_send.at[q], hs_recv.at[q], dpp,
        )
        cp.start()
        hcopies.append(cp)
    rlc = remote(replen, rl.at[d], rl_send, rl_recv, dpp)
    rlc.start()
    lnc = remote(ln.at[d], ln.at[d], ln_send, ln_recv, dpp)
    lnc.start()
    pend += hcopies + [rlc, lnc]
    for cp in firsts:
        cp.wait()

    def parts(h, ph):
        out = []
        for c in range(NC):
            if ph == 0:
                loads[c].wait()
            prt[h, c] = jnp.dot(
                xall[h], wv[:, c * vw : (c + 1) * vw], preferred_element_type=jnp.float32
            ).astype(jnp.bfloat16)
            cp = remote(prt.at[h, c], rpt.at[h, c], pt_send.at[ph, c], pt_recv.at[ph, c], dpp)
            cp.start()
            out.append(cp)
        return out

    own_parts = parts(d, 0)
    fws, fys, fyy = [], [], []
    yv = lax.rem(v + 2, 4)
    for q in range(2):
        hcopies[q].wait_recv()
        src = xall.at[p, piece(v, q)]
        cp = remote(src, src, fy_send.at[q], fy_recv.at[q], yp)
        cp.start()
        fyy.append(cp)
        cp = remote(src, src, fw_send.at[q], fw_recv.at[q], sib)
        cp.start()
        fws.append(cp)
    for q in range(2):
        fyy[q].wait_recv()
        src = xall.at[p, piece(yv, q)]
        cp = remote(src, src, ys_send.at[q], ys_recv.at[q], sib)
        cp.start()
        fys.append(cp)
    for cp in fws + fys:
        cp.wait_recv()
    other_parts = parts(p, 1)
    pend += fws + fys + fyy + own_parts + other_parts
    rlc.wait_recv()
    lnc.wait_recv()
    for h in range(2):
        for k in range(NC):
            ks = slice(k * cw, (k + 1) * cw)
            xt[ks, h * rows : (h + 1) * rows] = xall[h, :, ks].T
    cols_copy = pltpu.make_async_copy(xt, cols_out, o_sem.at[0])
    cols_copy.start()

    slot = lax.broadcasted_iota(jnp.int32, (seqs, slen, vw), 1).astype(jnp.float32)

    def forward(h, c):
        x = prt[h, c].astype(jnp.float32) + rpt[h, c].astype(jnp.float32)
        x = x + bias[:, c * vw : (c + 1) * vw]
        pos = jnp.maximum(x, 0.0)
        act = jnp.log1p(pos).reshape(seqs, slen, vw)
        lens = ln[h]
        live = slot < lens[:, None, :]
        act = jnp.where(live, act, 0.0)
        sq = act * act
        total = 1.0 + jnp.sum(sq * sq, axis=1)
        root = jnp.sqrt(jnp.sqrt(total))
        pool[h, c] = root - 1.0
        inv = 1.0 / root
        inv3 = inv * inv * inv
        f = sq * act * inv3[:, None, :] / (1.0 + pos.reshape(seqs, slen, vw))
        factor[h, c] = f.reshape(rows, vw)

    for c in range(NC):
        own_parts[c].wait_recv()
        forward(p, c)
    for c in range(NC):
        other_parts[c].wait_recv()
        forward(d, c)
        cs = slice(c * vw, (c + 1) * vw)
        mean = (
            jnp.sum(pool[0, c], axis=0, keepdims=True) + jnp.sum(pool[1, c], axis=0, keepdims=True)
        ) / (2 * seqs)
        mean_out[:, cs] = mean
        pooled_out[:, cs] = pool[d, c]
        bsum = jnp.zeros((1, vw), jnp.float32)
        for h in range(2):
            gp = rl[h, :, cs] + mean
            g = (factor[h, c].reshape(seqs, slen, vw) * gp[:, None, :]).reshape(rows, vw)
            bsum = bsum + jnp.sum(g, axis=0, keepdims=True)
            grad[h, :, cs] = g.astype(jnp.bfloat16)
        biasg_out[:, cs] = bsum

    grad_copy = pltpu.make_async_copy(grad, grad_out, o_sem.at[1])
    grad_copy.start()
    vr = 2 * rows // 4
    zr = vr // 4
    cc, yy, zz = [], [], []
    for c in range(NC):
        res = lax.dot_general(
            grad[...].reshape(2 * rows, NC * vw), wv[c * cw : (c + 1) * cw, :],
            (((1,), (1,)), ((), ())), preferred_element_type=jnp.float32,
        )
        for u in range(4):
            blk = res[u * vr : (u + 1) * vr]
            ipf[c, u % 2, u // 2] = blk
            s1[c, u % 2, u // 2] = blk.astype(jnp.bfloat16)
        cp = remote(s1.at[c, 1 - b], r1.at[c], c_send.at[c], c_recv.at[c], sib)
        cp.start()
        cc.append(cp)
    for c in range(NC):
        cc[c].wait_recv()
        s2[c] = (ipf[c, b, 1 - a] + r1[c, 1 - a].astype(jnp.float32)).astype(jnp.bfloat16)
        cp = remote(s2.at[c], r2.at[c], y_send.at[c], y_recv.at[c], yp)
        cp.start()
        yy.append(cp)
        k2[c] = ipf[c, b, a] + r1[c, a].astype(jnp.float32)
    for c in range(NC):
        yy[c].wait_recv()
        tot = (k2[c] + r2[c].astype(jnp.float32)).reshape(4, zr, cw)
        k3[c] = tot
        s3[c] = tot.astype(jnp.bfloat16)
        row = []
        for j in (1, 2, 3):
            to = lax.rem(rz + j, 4)
            cp = remote(
                s3.at[c, to], r3.at[c, j - 1], z_send.at[c, j - 1], z_recv.at[c, j - 1],
                {"replica": to},
            )
            cp.start()
            row.append(cp)
        zz.append(row)
    for c in range(NC):
        tot = k3[c, rz]
        for j in range(3):
            zz[c][j].wait_recv()
            tot = tot + r3[c, j].astype(jnp.float32)
        inp_out[:, c * cw : (c + 1) * cw] = tot
    for cp in pend + cc + yy + sum(zz, []):
        cp.wait_send()
    cols_copy.wait()
    grad_copy.wait()


def weight_kernel(cols, grad, pooled, mean, biasg, inp, out, pooled_o, mean_o, biasg_o, inp_o):
    kb = out.shape[0]
    at = pl.ds(pl.multiple_of(pl.program_id(0) * kb, kb), kb)
    out[...] = jnp.dot(cols[at, :], grad[...], preferred_element_type=jnp.float32)

    @pl.when(pl.program_id(0) == 0)
    def _():
        pooled_o[...] = pooled[...]
        mean_o[...] = mean[...]
        biasg_o[...] = biasg[...]
        inp_o[...] = inp[...]


def fused(hidden, head_weight, head_bias, rep_cotangent, lengths):
    rows, width = hidden.shape
    half, vc = head_weight.shape
    seqs = lengths.shape[0]
    vw, cw = vc // NC, half // NC
    vr = 2 * rows // 4
    zr = vr // 4
    bf, f32 = jnp.bfloat16, jnp.float32
    vm = pl.BlockSpec(memory_space=pltpu.VMEM)
    hbm = pl.BlockSpec(memory_space=pltpu.HBM)
    dma = pltpu.SemaphoreType.DMA
    sds = jax.ShapeDtypeStruct
    pooled, mean, biasg, cols, grad, inp = pl.pallas_call(
        head_kernel,
        out_shape=(
            sds((seqs, vc), f32), sds((1, vc), f32), sds((1, vc), f32),
            sds((half, 2 * rows), bf), sds((2, rows, vc), bf), sds((zr, half), f32),
        ),
        in_specs=[hbm] * 4 + [pl.BlockSpec(memory_space=pltpu.SMEM)],
        out_specs=(vm,) * 6,
        scratch_shapes=[
            pltpu.VMEM((half, vc), bf),
            pltpu.VMEM((1, vc), f32),
            pltpu.VMEM((2, rows, half), bf),
            pltpu.VMEM((half, 2 * rows), bf),
            pltpu.VMEM((2, seqs, vc), f32),
            pltpu.VMEM((2, seqs, vw), f32),
            pltpu.VMEM((2, NC, rows, vw), bf),
            pltpu.VMEM((2, NC, rows, vw), bf),
            pltpu.VMEM((2, NC, rows, vw), f32),
            pltpu.VMEM((2, NC, seqs, vw), f32),
            pltpu.VMEM((2, rows, vc), bf),
            pltpu.VMEM((NC, 2, 2, vr, cw), f32),
            pltpu.VMEM((NC, 2, 2, vr, cw), bf),
            pltpu.VMEM((NC, 2, vr, cw), bf),
            pltpu.VMEM((NC, vr, cw), f32),
            pltpu.VMEM((NC, vr, cw), bf),
            pltpu.VMEM((NC, vr, cw), bf),
            pltpu.VMEM((NC, 4, zr, cw), f32),
            pltpu.VMEM((NC, 4, zr, cw), bf),
            pltpu.VMEM((NC, 3, zr, cw), bf),
            dma((NC,)), dma((3,)), dma((2,)), dma((2,)), dma((2,)), dma((2,)), dma((2,)),
            dma((2,)), dma((2,)), dma((2,)), dma((2,)), dma, dma, dma, dma,
            dma((2, NC)), dma((2, NC)), dma((NC,)), dma((NC,)), dma((NC,)), dma((NC,)),
            dma((NC, 3)), dma((NC, 3)),
        ],
        compiler_params=pltpu.CompilerParams(
            collective_id=0, has_side_effects=True, vmem_limit_bytes=52 * 1024 * 1024
        ),
    )(hidden, head_weight, head_bias[None, :], rep_cotangent, lengths)
    kb = 256
    small = (pooled, mean, biasg, inp)
    whole = [pl.BlockSpec(x.shape, lambda i: (0, 0)) for x in small]
    weight_grad, pooled, mean, biasg, inp = pl.pallas_call(
        weight_kernel,
        grid=(half // kb,),
        out_shape=[sds((half, vc), f32)] + [sds(x.shape, f32) for x in small],
        in_specs=[vm] * 6,
        out_specs=[pl.BlockSpec((kb, vc), lambda i: (i, 0))] + whole,
        compiler_params=pltpu.CompilerParams(vmem_limit_bytes=40 * 1024 * 1024),
    )(cols, grad.reshape(2 * rows, vc), *small)
    return (pooled, mean[0], biasg[0], weight_grad, inp)


def solution(mesh):
    small = mesh.shape["dp"] == 2 and mesh.shape["vocab"] == 4 and mesh.shape["replica"] == 4
    placed = (
        P("dp", None),
        P("dp", ("vocab", "replica")),
        P(("vocab", "replica")),
        P("dp", ("vocab", "replica")),
        P("dp"),
    )
    return jax.shard_map(
        fused if small else per_device,
        mesh=mesh,
        in_specs=placed,
        out_specs=(
            P("dp", ("vocab", "replica")),
            P(("vocab", "replica")),
            P(("vocab", "replica")),
            P("dp", ("vocab", "replica")),
            P(("vocab", "replica"), "dp"),
        ),
        check_vma=False,
    )
```

```python
import jax
import jax.numpy as jnp
from jax import lax
from jax.experimental import pallas as pl
from jax.experimental.pallas import tpu as pltpu
from jax.sharding import PartitionSpec as P


def per_device(hidden, head_weight, head_bias, rep_cotangent, lengths):
    dp_count = lax.axis_size("dp")
    vocab_cols = head_weight.shape[1]
    columns = lax.all_to_all(hidden, "dp", split_axis=1, concat_axis=0, tiled=True)
    rep_all = lax.all_gather(rep_cotangent, "dp", axis=0, tiled=True)
    lengths_all = lax.all_gather(lengths.astype(jnp.float32), "dp", axis=0, tiled=True)
    seq_count = lengths_all.shape[0]
    tok_rows = columns.shape[0]
    seq_len = tok_rows // seq_count
    part = jnp.dot(columns, head_weight, preferred_element_type=jnp.float32).astype(jnp.bfloat16)
    part = lax.optimization_barrier(part)
    if dp_count == 2:
        other = lax.ppermute(part, "dp", [(0, 1), (1, 0)])
        running = part.astype(jnp.float32) + other.astype(jnp.float32)
    else:
        parts = lax.all_gather(part, "dp", axis=0, tiled=False)
        running = jnp.sum(parts.astype(jnp.float32), axis=0)
    logits = running + head_bias[None, :]
    positive = jnp.maximum(logits, 0.0)
    grid = jnp.log1p(positive).reshape(seq_count, seq_len, vocab_cols)
    slot = jnp.arange(seq_len, dtype=jnp.float32)
    live = (slot[None, :] < lengths_all[:, None]).astype(jnp.float32)[:, :, None]
    squared = grid * grid
    total = 1.0 + jnp.sum(live * squared * squared, axis=1)
    pooled = total**0.25 - 1.0
    factor = (
        live * squared * grid * (total ** (-0.75))[:, None, :]
        / (1.0 + positive.reshape(seq_count, seq_len, vocab_cols))
    )
    term_mean = jnp.sum(pooled, axis=0) / seq_count
    grad_pooled = rep_all + term_mean[None, :]
    grad_logits = (factor * grad_pooled[:, None, :]).reshape(tok_rows, vocab_cols)
    bias_grad = jnp.sum(grad_logits, axis=0)
    grad_round = grad_logits.astype(jnp.bfloat16)
    input_part = jnp.einsum("tv,kv->tk", grad_round, head_weight, preferred_element_type=jnp.float32)
    input_grad = lax.psum_scatter(input_part, ("vocab", "replica"), scatter_dimension=0, tiled=True)
    weight_grad = jnp.einsum("tk,tv->kv", columns, grad_round, preferred_element_type=jnp.float32)
    own = seq_count // dp_count
    pooled_own = lax.dynamic_slice_in_dim(pooled, lax.axis_index("dp") * own, own, 0)
    return (pooled_own, term_mean, bias_grad, weight_grad, input_grad)


NC = 4
RC = 8
MESH = pl.DeviceIdType.MESH


def head_kernel(
    hidden, weight, bias_in, replen, lengths,
    pooled_out, mean_out, biasg_out, cols_out, grad_out, inp_out,
    wv, bias, xall, xt, rl, ln, prt, rpt, factor, pool, grad, ipf, s1, r1, k2, s2, r2, k3, s3, r3,
    w_sem, l_sem, o_sem, hs_send, hs_recv, fw_send, fw_recv, fy_send, fy_recv, ys_send, ys_recv, ln_send, ln_recv, rl_send, rl_recv, pt_send, pt_recv,
    c_send, c_recv, y_send, y_recv, z_send, z_recv,
):
    v, d, rz = lax.axis_index("vocab"), lax.axis_index("dp"), lax.axis_index("replica")
    p = 1 - d
    b, a = lax.rem(v, 2), v // 2
    sib = {"vocab": v + 1 - 2 * b}
    yp = {"vocab": lax.rem(v + 2, 4)}
    dpp = {"dp": p}
    half = hidden.shape[1] // 2
    cw = half // RC
    vw = wv.shape[1] // NC
    rows = hidden.shape[0]
    seqs = rl.shape[1]
    slen = rows // seqs
    hr = rows // 8

    def remote(src, dst, ss, rs, dev):
        return pltpu.make_async_remote_copy(
            src_ref=src, dst_ref=dst, send_sem=ss, recv_sem=rs, device_id=dev, device_id_type=MESH
        )

    firsts = [
        pltpu.make_async_copy(
            hidden.at[:, pl.ds(pl.multiple_of(d * half, half), half)], xall.at[d], l_sem.at[0]
        ),
        pltpu.make_async_copy(replen, rl.at[d], l_sem.at[1]),
        pltpu.make_async_copy(bias_in, bias, l_sem.at[2]),
    ]
    for cp in firsts:
        cp.start()
    for i in range(seqs):
        ln[d, i : i + 1, :] = jnp.full((1, vw), lengths[i].astype(jnp.float32))
    loads = []
    for c in range(NC):
        cp = pltpu.make_async_copy(
            weight.at[:, pl.ds(c * vw, vw)], wv.at[:, pl.ds(c * vw, vw)], w_sem.at[c]
        )
        cp.start()
        loads.append(cp)
    barrier = pltpu.get_barrier_semaphore()
    zps = [{"replica": lax.rem(rz + j, 4)} for j in (1, 2, 3)]
    for dev in [sib, yp, dpp] + zps:
        pl.semaphore_signal(barrier, inc=1, device_id=dev, device_id_type=MESH)
    pl.semaphore_wait(barrier, 6)

    pend = []
    hcopies = []

    def piece(who, q):
        return pl.ds(pl.multiple_of(who * (2 * hr) + q * hr, hr), hr)

    for q in range(2):
        cp = remote(
            hidden.at[piece(v, q), pl.ds(pl.multiple_of(p * half, half), half)],
            xall.at[d, piece(v, q)], hs_send.at[q], hs_recv.at[q], dpp,
        )
        cp.start()
        hcopies.append(cp)
    rlc = remote(replen, rl.at[d], rl_send, rl_recv, dpp)
    rlc.start()
    lnc = remote(ln.at[d], ln.at[d], ln_send, ln_recv, dpp)
    lnc.start()
    pend += hcopies + [rlc, lnc]
    for cp in firsts:
        cp.wait()

    def parts(h, ph):
        out = []
        for c in range(NC):
            if ph == 0:
                loads[c].wait()
            prt[h, c] = jnp.dot(
                xall[h], wv[:, c * vw : (c + 1) * vw], preferred_element_type=jnp.float32
            ).astype(jnp.bfloat16)
            cp = remote(prt.at[h, c], rpt.at[h, c], pt_send.at[ph, c], pt_recv.at[ph, c], dpp)
            cp.start()
            out.append(cp)
        return out

    own_parts = parts(d, 0)
    fws, fys, fyy = [], [], []
    yv = lax.rem(v + 2, 4)
    for q in range(2):
        hcopies[q].wait_recv()
        src = xall.at[p, piece(v, q)]
        cp = remote(src, src, fy_send.at[q], fy_recv.at[q], yp)
        cp.start()
        fyy.append(cp)
        cp = remote(src, src, fw_send.at[q], fw_recv.at[q], sib)
        cp.start()
        fws.append(cp)
    for q in range(2):
        fyy[q].wait_recv()
        src = xall.at[p, piece(yv, q)]
        cp = remote(src, src, ys_send.at[q], ys_recv.at[q], sib)
        cp.start()
        fys.append(cp)
    for cp in fws + fys:
        cp.wait_recv()
    other_parts = parts(p, 1)
    pend += fws + fys + fyy + own_parts + other_parts
    rlc.wait_recv()
    lnc.wait_recv()
    for h in range(2):
        for k in range(RC):
            ks = slice(k * cw, (k + 1) * cw)
            xt[ks, h * rows : (h + 1) * rows] = xall[h, :, ks].T
    cols_copy = pltpu.make_async_copy(xt, cols_out, o_sem.at[0])
    cols_copy.start()

    slot = lax.broadcasted_iota(jnp.int32, (seqs, slen, vw), 1).astype(jnp.float32)

    def forward(h, c):
        x = prt[h, c].astype(jnp.float32) + rpt[h, c].astype(jnp.float32)
        x = x + bias[:, c * vw : (c + 1) * vw]
        pos = jnp.maximum(x, 0.0)
        act = jnp.log1p(pos).reshape(seqs, slen, vw)
        lens = ln[h]
        live = slot < lens[:, None, :]
        act = jnp.where(live, act, 0.0)
        sq = act * act
        total = 1.0 + jnp.sum(sq * sq, axis=1)
        root = jnp.sqrt(jnp.sqrt(total))
        pool[h, c] = root - 1.0
        inv = 1.0 / root
        inv3 = inv * inv * inv
        f = sq * act * inv3[:, None, :] / (1.0 + pos.reshape(seqs, slen, vw))
        factor[h, c] = f.reshape(rows, vw)

    for c in range(NC):
        own_parts[c].wait_recv()
        forward(p, c)
    for c in range(NC):
        other_parts[c].wait_recv()
        forward(d, c)
        cs = slice(c * vw, (c + 1) * vw)
        mean = (
            jnp.sum(pool[0, c], axis=0, keepdims=True) + jnp.sum(pool[1, c], axis=0, keepdims=True)
        ) / (2 * seqs)
        mean_out[:, cs] = mean
        pooled_out[:, cs] = pool[d, c]
        bsum = jnp.zeros((1, vw), jnp.float32)
        for h in range(2):
            gp = rl[h, :, cs] + mean
            g = (factor[h, c].reshape(seqs, slen, vw) * gp[:, None, :]).reshape(rows, vw)
            bsum = bsum + jnp.sum(g, axis=0, keepdims=True)
            grad[h, :, cs] = g.astype(jnp.bfloat16)
        biasg_out[:, cs] = bsum

    grad_copy = pltpu.make_async_copy(grad, grad_out, o_sem.at[1])
    grad_copy.start()
    vr = 2 * rows // 4
    zr = vr // 4
    cc, yy, zz = [], [], []
    for c in range(RC):
        res = lax.dot_general(
            grad[...].reshape(2 * rows, NC * vw), wv[c * cw : (c + 1) * cw, :],
            (((1,), (1,)), ((), ())), preferred_element_type=jnp.float32,
        )
        for u in range(4):
            blk = res[u * vr : (u + 1) * vr]
            ipf[c, u % 2, u // 2] = blk
            s1[c, u % 2, u // 2] = blk.astype(jnp.bfloat16)
        cp = remote(s1.at[c, 1 - b], r1.at[c], c_send.at[c], c_recv.at[c], sib)
        cp.start()
        cc.append(cp)
    for c in range(RC):
        cc[c].wait_recv()
        s2[c] = (ipf[c, b, 1 - a] + r1[c, 1 - a].astype(jnp.float32)).astype(jnp.bfloat16)
        cp = remote(s2.at[c], r2.at[c], y_send.at[c], y_recv.at[c], yp)
        cp.start()
        yy.append(cp)
        k2[c] = ipf[c, b, a] + r1[c, a].astype(jnp.float32)
    for c in range(RC):
        yy[c].wait_recv()
        tot = (k2[c] + r2[c].astype(jnp.float32)).reshape(4, zr, cw)
        k3[c] = tot
        s3[c] = tot.astype(jnp.bfloat16)
        row = []
        for j in (1, 2, 3):
            to = lax.rem(rz + j, 4)
            cp = remote(
                s3.at[c, to], r3.at[c, j - 1], z_send.at[c, j - 1], z_recv.at[c, j - 1],
                {"replica": to},
            )
            cp.start()
            row.append(cp)
        zz.append(row)
    for c in range(RC):
        tot = k3[c, rz]
        for j in range(3):
            zz[c][j].wait_recv()
            tot = tot + r3[c, j].astype(jnp.float32)
        inp_out[:, c * cw : (c + 1) * cw] = tot
    for cp in pend + cc + yy + sum(zz, []):
        cp.wait_send()
    cols_copy.wait()
    grad_copy.wait()


def weight_kernel(cols, grad, pooled, mean, biasg, inp, out, pooled_o, mean_o, biasg_o, inp_o):
    kb = out.shape[0]
    at = pl.ds(pl.multiple_of(pl.program_id(0) * kb, kb), kb)
    out[...] = jnp.dot(cols[at, :], grad[...], preferred_element_type=jnp.float32)

    @pl.when(pl.program_id(0) == 0)
    def _():
        pooled_o[...] = pooled[...]
        mean_o[...] = mean[...]
        biasg_o[...] = biasg[...]
        inp_o[...] = inp[...]


def fused(hidden, head_weight, head_bias, rep_cotangent, lengths):
    rows, width = hidden.shape
    half, vc = head_weight.shape
    seqs = lengths.shape[0]
    vw, cw = vc // NC, half // RC
    vr = 2 * rows // 4
    zr = vr // 4
    bf, f32 = jnp.bfloat16, jnp.float32
    vm = pl.BlockSpec(memory_space=pltpu.VMEM)
    hbm = pl.BlockSpec(memory_space=pltpu.HBM)
    dma = pltpu.SemaphoreType.DMA
    sds = jax.ShapeDtypeStruct
    pooled, mean, biasg, cols, grad, inp = pl.pallas_call(
        head_kernel,
        out_shape=(
            sds((seqs, vc), f32), sds((1, vc), f32), sds((1, vc), f32),
            sds((half, 2 * rows), bf), sds((2, rows, vc), bf), sds((zr, half), f32),
        ),
        in_specs=[hbm] * 4 + [pl.BlockSpec(memory_space=pltpu.SMEM)],
        out_specs=(vm,) * 6,
        scratch_shapes=[
            pltpu.VMEM((half, vc), bf),
            pltpu.VMEM((1, vc), f32),
            pltpu.VMEM((2, rows, half), bf),
            pltpu.VMEM((half, 2 * rows), bf),
            pltpu.VMEM((2, seqs, vc), f32),
            pltpu.VMEM((2, seqs, vw), f32),
            pltpu.VMEM((2, NC, rows, vw), bf),
            pltpu.VMEM((2, NC, rows, vw), bf),
            pltpu.VMEM((2, NC, rows, vw), f32),
            pltpu.VMEM((2, NC, seqs, vw), f32),
            pltpu.VMEM((2, rows, vc), bf),
            pltpu.VMEM((RC, 2, 2, vr, cw), f32),
            pltpu.VMEM((RC, 2, 2, vr, cw), bf),
            pltpu.VMEM((RC, 2, vr, cw), bf),
            pltpu.VMEM((RC, vr, cw), f32),
            pltpu.VMEM((RC, vr, cw), bf),
            pltpu.VMEM((RC, vr, cw), bf),
            pltpu.VMEM((RC, 4, zr, cw), f32),
            pltpu.VMEM((RC, 4, zr, cw), bf),
            pltpu.VMEM((RC, 3, zr, cw), bf),
            dma((NC,)), dma((3,)), dma((2,)), dma((2,)), dma((2,)), dma((2,)), dma((2,)),
            dma((2,)), dma((2,)), dma((2,)), dma((2,)), dma, dma, dma, dma,
            dma((2, NC)), dma((2, NC)), dma((RC,)), dma((RC,)), dma((RC,)), dma((RC,)),
            dma((RC, 3)), dma((RC, 3)),
        ],
        compiler_params=pltpu.CompilerParams(
            collective_id=0, has_side_effects=True, vmem_limit_bytes=52 * 1024 * 1024
        ),
    )(hidden, head_weight, head_bias[None, :], rep_cotangent, lengths)
    kb = 256
    small = (pooled, mean, biasg, inp)
    whole = [pl.BlockSpec(x.shape, lambda i: (0, 0)) for x in small]
    weight_grad, pooled, mean, biasg, inp = pl.pallas_call(
        weight_kernel,
        grid=(half // kb,),
        out_shape=[sds((half, vc), f32)] + [sds(x.shape, f32) for x in small],
        in_specs=[vm] * 6,
        out_specs=[pl.BlockSpec((kb, vc), lambda i: (i, 0))] + whole,
        compiler_params=pltpu.CompilerParams(vmem_limit_bytes=40 * 1024 * 1024),
    )(cols, grad.reshape(2 * rows, vc), *small)
    return (pooled, mean[0], biasg[0], weight_grad, inp)


def solution(mesh):
    small = mesh.shape["dp"] == 2 and mesh.shape["vocab"] == 4 and mesh.shape["replica"] == 4
    placed = (
        P("dp", None),
        P("dp", ("vocab", "replica")),
        P(("vocab", "replica")),
        P("dp", ("vocab", "replica")),
        P("dp"),
    )
    return jax.shard_map(
        fused if small else per_device,
        mesh=mesh,
        in_specs=placed,
        out_specs=(
            P("dp", ("vocab", "replica")),
            P(("vocab", "replica")),
            P(("vocab", "replica")),
            P("dp", ("vocab", "replica")),
            P(("vocab", "replica"), "dp"),
        ),
        check_vma=False,
    )
```
